512 devices in a mesh: queue: 32 (over z_lo, x, core), dp: 16 (over y, z_hi).
Axes of the slice: x: 4, y: 8, z: 8 (z_hi: 2, z_lo: 4; z = z_hi * 4 + z_lo), core: 2. Of those that a mesh axis runs over, the one named last changes fastest.
Arguments:
- stream: bfloat16 [57344, 1536], P(('queue', 'dp')), may hold values from -6 to 6
- incoming: bfloat16 [1792, 1536], P('dp'), may hold values from -6 to 6
- levels: int32 [2, 32], replicated, may hold values from 0 to 31
- bounds: int32 [512, 2], P(('queue', 'dp')), may hold values from 0 to 512, as said below
- mod_table: float32 [32, 3, 1536], replicated, may hold values from -3 to 3
- w_query: bfloat16 [1536, 1536], P('dp'), may hold values from -0.15625 to 0.15625
- w_key: bfloat16 [1536, 1536], P('dp'), may hold values from -0.15625 to 0.15625
- w_value: bfloat16 [1536, 1536], P('dp'), may hold values from -0.15625 to 0.15625
- gain_query: float32 [1536], replicated, may hold values from 0.5 to 7
- gain_key: float32 [1536], replicated, may hold values from 0.5 to 7
Outputs:
- queue_state: bfloat16 [57344, 1536], P(('queue', 'dp'))
The draws below stay inside these ranges and needn't reach their ends.
Inputs may be any that keep to these rules, and one draw needn't show every extreme that they name: bounds[f, 0] is f - 1 or f, and bounds[f, 1] is f + 1 or f + 2, clipped to 0 and 512.
All inputs are finite; a program needn't handle non-finite values.
Results may differ from the reference program's by a relative error of at most 0.039.
Values may be sent and summed in bfloat16 or wider, within the bound.
No kernel may reach another device: no remote copies, remote signals or barrier semaphores. Data moves between devices by JAX's collectives and lax.ppermute only.
A program may use at most 64 MiB of HBM per device.

```python
import math
import jax
import jax.numpy as jnp
from jax import lax

HEADS = 12
HEAD_DIM = 128
D = 1536
TOK_DEV = 112
LEVELS = 32
STEPS = 2
SECTIONS = 32
NFRAMES = 512
GROUP = 1792
TOKENS = 57344


def draw_bounds(key, part):
    key = jax.random.fold_in(key, 7)
    behind = jax.random.randint(jax.random.fold_in(key, 1), (NFRAMES,), 0, 2)
    ahead = jax.random.randint(jax.random.fold_in(key, 2), (NFRAMES,), 0, 2)
    frames = jnp.arange(NFRAMES, dtype=jnp.int32)
    lower = jnp.maximum(frames - behind, 0)
    upper = jnp.minimum(frames + 1 + ahead, NFRAMES)
    return jnp.stack([lower, upper], axis=1).astype(jnp.int32)


def gain_values(key, lowest, highest):
    uniform_part = jax.random.uniform(key, (HEADS * HEAD_DIM,), jnp.float32)
    return jnp.exp(math.log(lowest) + (math.log(highest) - math.log(lowest)) * uniform_part)


def draw_gain_query(key, part):
    key = jax.random.fold_in(key, 11)
    return gain_values(key, 0.5, 2.0)


def draw_gain_key(key, part):
    key = jax.random.fold_in(key, 13)
    return gain_values(key, 0.5, 2.0)


def set_ends(entries, rng, least, top_value):
    dims = entries.shape
    index_at = [jax.random.randint(jax.random.fold_in(rng, axis), (), 0, dims[axis]) for axis in range(len(dims))]
    entries = entries.at[tuple(index_at)].set(least)
    longest = dims.index(max(dims))
    index_at[longest] = (index_at[longest] + 1) % dims[longest]
    return entries.at[tuple(index_at)].set(top_value)


def block_scale(own_key, extent, split, low, high):
    def one(position, blocks):
        steps = jax.random.uniform(jax.random.fold_in(jax.random.fold_in(own_key, 6), position), (blocks,), jnp.float32, low / len(split), high / len(split))
        return jnp.repeat(jnp.exp(steps), extent[position] // blocks).reshape((-1,) + (1,) * (len(extent) - position - 1))

    factor_of = one(*split[0])
    for cut in split[1:]:
        factor_of = factor_of * one(*cut)
    return factor_of


def gaussian(own_key, shape, width, reach, shards=(), held_as=jnp.bfloat16):
    entries = jax.random.normal(own_key, shape, jnp.float32) * width
    if len(shards) > 0:
        entries = block_scale(own_key, shape, shards, -0.22, 0.18) * entries
    return jnp.clip(entries, min=-reach, max=reach).astype(held_as)


def setup_inputs(seed: int = 0) -> dict:
    arg_keys = jax.random.split(jax.random.key(seed), 11)
    return {
        "stream": gaussian(arg_keys[0], (TOKENS, D), 1.0, 6.0, ((0, 512),)),
        "incoming": gaussian(arg_keys[1], (GROUP, D), 1.0, 6.0, ((0, 16),)),
        "levels": set_ends(jax.random.randint(arg_keys[2], (STEPS, SECTIONS), 0, LEVELS), jax.random.fold_in(arg_keys[2], 1), 0, LEVELS - 1).astype(jnp.int32),
        "bounds": draw_bounds(jax.random.fold_in(arg_keys[10], 71), 0),
        "mod_table": gaussian(arg_keys[4], (LEVELS, 3, D), 0.5, 3.0, (), jnp.float32),
        "w_query": gaussian(arg_keys[5], (D, D), D ** -0.5, 0.15625, ((0, 16),)),
        "w_key": gaussian(arg_keys[6], (D, D), D ** -0.5, 0.15625, ((0, 16),)),
        "w_value": gaussian(arg_keys[7], (D, D), D ** -0.5, 0.15625, ((0, 16),)),
        "gain_query": draw_gain_query(jax.random.fold_in(arg_keys[10], 71), 0),
        "gain_key": draw_gain_key(jax.random.fold_in(arg_keys[10], 71), 0),
    }


epsilon = 1e-06

def layer_norm(values):
    average = lax.optimization_barrier(jnp.mean(values, axis=-1, keepdims=True))
    centred = values - average
    spread = lax.optimization_barrier(jnp.mean(centred * centred, axis=-1, keepdims=True))
    return centred * lax.rsqrt(spread + epsilon)

def rms_norm(values, gain):
    power = lax.optimization_barrier(jnp.mean(values * values, axis=-1, keepdims=True))
    return values * lax.rsqrt(power + epsilon) * gain

def denoise(stream, level_row, mod_table, w_query, w_key, w_value, gain_query, gain_key, bounds):
    model_width = HEADS * HEAD_DIM
    modulation = mod_table[level_row]
    widened = stream.astype(jnp.float32).reshape(SECTIONS, GROUP, model_width)
    normed = layer_norm(widened) * (1.0 + modulation[:, 1][:, None, :]) + modulation[:, 0][:, None, :]
    flat = normed.astype(jnp.bfloat16).reshape(TOKENS, model_width)
    query = rms_norm(jnp.dot(flat, w_query, preferred_element_type=jnp.float32), gain_query).astype(jnp.bfloat16)
    key_all = rms_norm(jnp.dot(flat, w_key, preferred_element_type=jnp.float32), gain_key).astype(jnp.bfloat16)
    value_all = jnp.dot(flat, w_value, preferred_element_type=jnp.float32).astype(jnp.bfloat16)
    query = query.reshape(NFRAMES, TOK_DEV, HEADS, HEAD_DIM)
    padding = ((1, 1), (0, 0), (0, 0), (0, 0))
    key_pad = jnp.pad(key_all.reshape(NFRAMES, TOK_DEV, HEADS, HEAD_DIM), padding)
    value_pad = jnp.pad(value_all.reshape(NFRAMES, TOK_DEV, HEADS, HEAD_DIM), padding)

    def attend(frame_idx):
        query_block = lax.dynamic_index_in_dim(query, frame_idx, 0, keepdims=False)
        key_block = lax.dynamic_slice_in_dim(key_pad, frame_idx, 3, 0).reshape(3 * TOK_DEV, HEADS, HEAD_DIM)
        value_block = lax.dynamic_slice_in_dim(value_pad, frame_idx, 3, 0).reshape(3 * TOK_DEV, HEADS, HEAD_DIM)
        scores = jnp.einsum('qhd,khd->hqk', query_block.astype(jnp.float32), key_block.astype(jnp.float32)) * HEAD_DIM ** (-0.5)
        key_frame = frame_idx - 1 + jnp.arange(3 * TOK_DEV, dtype=jnp.int32) // TOK_DEV
        window = lax.dynamic_index_in_dim(bounds, frame_idx, 0, keepdims=False)
        allowed = (key_frame >= window[0]) & (key_frame < window[1])
        scores = jnp.where(allowed[None, None, :], scores, jnp.float32(-1e+30))
        peak = lax.optimization_barrier(jnp.max(scores, axis=-1, keepdims=True))
        weights = jnp.exp(scores - peak)
        total = lax.optimization_barrier(jnp.sum(weights, axis=-1, keepdims=True))
        probs = (weights / total).astype(jnp.bfloat16)
        return jnp.einsum('hqk,khd->qhd', probs.astype(jnp.float32), value_block.astype(jnp.float32)).astype(jnp.bfloat16)
    attended = lax.map(attend, jnp.arange(NFRAMES, dtype=jnp.int32))
    attended = attended.reshape(SECTIONS, GROUP, model_width)
    advanced = widened + modulation[:, 2][:, None, :] * attended.astype(jnp.float32)
    return advanced.astype(jnp.bfloat16).reshape(TOKENS, model_width)

def reference(stream, incoming, levels, bounds, mod_table, w_query, w_key, w_value, gain_query, gain_key):
    model_width = HEADS * HEAD_DIM
    first = denoise(stream, levels[0], mod_table, w_query, w_key, w_value, gain_query, gain_key, bounds)
    sectioned = first.reshape(SECTIONS, GROUP, model_width)
    moved = jnp.concatenate([incoming.reshape(1, GROUP, model_width), sectioned[:-1]], axis=0)
    moved = moved.reshape(TOKENS, model_width)
    return denoise(moved, levels[1], mod_table, w_query, w_key, w_value, gain_query, gain_key, bounds)
```

```python
import functools

import jax
import jax.numpy as jnp
from jax import lax
from jax.experimental import pallas as pl
from jax.experimental.pallas import tpu as pltpu
from jax.sharding import Mesh, PartitionSpec as P

HEADS = 12
HEAD_DIM = 128
D = HEADS * HEAD_DIM
BAND = 112
PER_SECTION = 16
SECTIONS = 32
DEVICES = SECTIONS * PER_SECTION
ROWS = D // PER_SECTION
HALF = 3 * D // 2
TILE = 256
FLAGS = 16
EPSILON = 1e-06
SHAPE = (4, 4, 2, 8, 2)
AXES = ("zl", "x", "core", "y", "zh")


def layer_norm(values):
    average = jnp.mean(values, axis=-1, keepdims=True)
    centred = values - average
    spread = jnp.mean(centred * centred, axis=-1, keepdims=True)
    return centred * lax.rsqrt(spread + EPSILON)


def attend(query, key, value, query_rows, first, bias):
    scores = lax.dot_general(
        query[query_rows : query_rows + BAND],
        key[first : first + 3 * BAND],
        (((1,), (1,)), ((), ())),
        preferred_element_type=jnp.float32,
    )
    scores = scores + bias
    peak = jnp.max(scores, axis=-1, keepdims=True)
    weights = jnp.exp2((scores - peak) * (HEAD_DIM**-0.5 * 1.4426950408889634))
    total = jnp.sum(weights, axis=-1, keepdims=True)
    mixed = jnp.dot(
        weights.astype(jnp.bfloat16),
        value[first : first + 3 * BAND],
        preferred_element_type=jnp.float32,
    )
    return (mixed / total).astype(jnp.bfloat16)


def compute(
    place,
    normed_ref,
    window_ref,
    bias_first_ref,
    gate_first_ref,
    mod_ref,
    bias_second_ref,
    gain_query_ref,
    gain_key_ref,
    own_ref,
    own_across_ref,
    far_ref,
    far_across_ref,
    out_ref,
    weights,
    query,
    key,
    value,
    advanced,
    normed,
    sem,
):
    frame, core, zh = place[0], place[1], place[2]
    copies = []
    for part, ref in enumerate((own_ref, far_ref, own_across_ref, far_across_ref)):
        half = core if part < 2 else 1 - core
        side = zh if part % 2 == 0 else 1 - zh
        columns = pl.ds(pl.multiple_of(half * HALF, 128), HALF)
        for y in range(8):
            rows = pl.ds(pl.multiple_of((2 * y + side) * ROWS, 32), ROWS)
            copies.append(
                pltpu.make_async_copy(
                    ref.at[pl.ds(y * ROWS, ROWS), :],
                    weights.at[rows, columns],
                    sem.at[part * 8 + y],
                )
            )
    for copy in copies:
        copy.start()
    for copy in copies:
        copy.wait()

    def project(source, bands):
        rows = bands * BAND
        inner = (bands - 2) * BAND

        def tile(index, rows_of):
            columns = pl.ds(pl.multiple_of(index * TILE, TILE), TILE)
            return jnp.dot(
                source[rows_of, :], weights[:, columns], preferred_element_type=jnp.float32
            )

        def folded(product):
            squares = product * product
            return squares[:, :128] + squares[:, 128:]

        def query_tile(i, power):
            product = tile(i, pl.ds(BAND, inner))
            query[:inner, pl.ds(pl.multiple_of(i * TILE, TILE), TILE)] = product
            return power + folded(product)

        def key_tile(i, power):
            product = tile(i + D // TILE, pl.ds(0, rows))
            key[:rows, pl.ds(pl.multiple_of(i * TILE, TILE), TILE)] = product
            return power + folded(product)

        def value_tile(i, carry):
            product = tile(i + 2 * (D // TILE), pl.ds(0, rows))
            value[:rows, pl.ds(pl.multiple_of(i * TILE, TILE), TILE)] = product.astype(jnp.bfloat16)
            return carry

        tiles = D // TILE
        query_power = lax.fori_loop(0, tiles, query_tile, jnp.zeros((inner, 128), jnp.float32))
        key_power = lax.fori_loop(0, tiles, key_tile, jnp.zeros((rows, 128), jnp.float32))
        lax.fori_loop(0, tiles, value_tile, 0)
        norm = lambda power: lax.rsqrt(jnp.sum(power, axis=-1, keepdims=True) * (1.0 / D) + EPSILON)
        return norm(query_power), norm(key_power)

    def heads_of(bands, query_norm, key_norm, biases, finish):
        rows = bands * BAND
        inner = (bands - 2) * BAND

        def one_head(h, carry):
            lanes = pl.ds(pl.multiple_of(h * HEAD_DIM, HEAD_DIM), HEAD_DIM)
            head_query = (query[:inner, lanes] * query_norm * gain_query_ref[:, lanes]).astype(jnp.bfloat16)
            head_key = (key[:rows, lanes] * key_norm * gain_key_ref[:, lanes]).astype(jnp.bfloat16)
            head_value = value[:rows, lanes]
            for band in range(bands - 2):
                attended = attend(head_query, head_key, head_value, band * BAND, band * BAND, biases[band])
                finish(band, lanes, attended.astype(jnp.float32))
            return carry

        lax.fori_loop(0, HEADS, one_head, 0)

    query_norm, key_norm = project(normed_ref, 5)

    def finish_first(band, lanes, attended):
        rows = slice(band * BAND, (band + 1) * BAND)
        held = window_ref[rows, lanes].astype(jnp.float32)
        moved = (held + gate_first_ref[band : band + 1, lanes] * attended).astype(jnp.bfloat16)
        advanced[rows, lanes] = jnp.where(frame + band - 1 < PER_SECTION, window_ref[rows, lanes], moved)

    heads_of(5, query_norm, key_norm, [bias_first_ref[b : b + 1, :] for b in range(3)], finish_first)

    for band in range(3):
        rows = slice(band * BAND, (band + 1) * BAND)
        level = layer_norm(advanced[rows, :].astype(jnp.float32))
        normed[rows, :] = (
            level * (1.0 + mod_ref[3 * band + 1 : 3 * band + 2, :]) + mod_ref[3 * band : 3 * band + 1, :]
        ).astype(jnp.bfloat16)

    query_norm, key_norm = project(normed, 3)

    def finish_second(band, lanes, attended):
        held = advanced[BAND : 2 * BAND, lanes].astype(jnp.float32)
        out_ref[:, lanes] = (held + mod_ref[5:6, lanes] * attended).astype(jnp.bfloat16)

    heads_of(3, query_norm, key_norm, [bias_second_ref[0:1, :]], finish_second)


def bias_of(flags):
    lane = jnp.arange(3 * BAND, dtype=jnp.int32) // BAND
    closed = jnp.where(lane == 0, flags[:, 0:1], jnp.where(lane == 2, flags[:, 1:2], 0.0))
    return closed * -1e30


def shards(
    stream, incoming, levels, bounds, mod_table, w_query, w_key, w_value, gain_query, gain_key
):
    core = lax.axis_index("core")
    zh = lax.axis_index("zh")
    frame = lax.axis_index(AXES)

    packed = jnp.concatenate([w_query, w_key, w_value], axis=1)
    half = jnp.where(core == 0, packed[:, :HALF], packed[:, HALF:])
    across = lambda block: lax.ppermute(block, "core", [(0, 1), (1, 0)])
    opposite = lax.ppermute(half, "zh", [(0, 1), (1, 0)])
    own = lax.all_gather(half, "y", axis=0, tiled=True)
    far = lax.all_gather(opposite, "y", axis=0, tiled=True)
    own_across = across(own)
    far_across = across(far)

    flag_pair = jnp.stack([bounds[0, 0] >= frame, bounds[0, 1] <= frame + 1]).astype(jnp.bfloat16)
    flag_rows = jnp.zeros((FLAGS, D), jnp.bfloat16).at[:2, :].set(flag_pair[:, None])
    bands, flags = [], []
    for k in range(-2, 3):
        block = stream
        if abs(k) < 2:
            wraps = frame + PER_SECTION - k >= DEVICES
            block = jnp.concatenate([jnp.where(wraps, incoming, stream), flag_rows], axis=0)
        route = [(d, (d + PER_SECTION - k) % DEVICES) for d in range(DEVICES)]
        got = lax.ppermute(block, AXES, route)
        bands.append(got[:BAND])
        if abs(k) < 2:
            flags.append(got[BAND : BAND + 2, 0].astype(jnp.float32))
    bias_first = bias_of(jnp.stack(flags))
    bias_second = bias_of(flag_pair.astype(jnp.float32)[None, :])

    def rows_at(step, band):
        section = jnp.clip(band // PER_SECTION, 0, SECTIONS - 1)
        return lax.dynamic_index_in_dim(mod_table, levels[step, section], 0, keepdims=False)

    first = [rows_at(0, frame - PER_SECTION + k) for k in range(-2, 3)]
    second = [rows_at(1, frame + k) for k in range(-1, 2)]
    normed = jnp.concatenate(
        [
            (layer_norm(band.astype(jnp.float32)) * (1.0 + row[1][None, :]) + row[0][None, :]).astype(
                jnp.bfloat16
            )
            for band, row in zip(bands, first)
        ],
        axis=0,
    )
    window = jnp.concatenate(bands[1:4], axis=0)
    gate_first = jnp.stack([row[2] for row in first[1:4]])
    mod_second = jnp.concatenate(second, axis=0)
    place = jnp.stack([frame, core, zh]).astype(jnp.int32)

    vmem = pl.BlockSpec(memory_space=pltpu.VMEM)
    anywhere = pl.BlockSpec(memory_space=pl.ANY)
    return pl.pallas_call(
        compute,
        out_shape=jax.ShapeDtypeStruct((BAND, D), jnp.bfloat16),
        in_specs=[pl.BlockSpec(memory_space=pltpu.SMEM)] + [vmem] * 8 + [anywhere] * 4,
        out_specs=vmem,
        scratch_shapes=[
            pltpu.VMEM((D, 3 * D), jnp.bfloat16),
            pltpu.VMEM((3 * BAND, D), jnp.float32),
            pltpu.VMEM((5 * BAND, D), jnp.float32),
            pltpu.VMEM((5 * BAND, D), jnp.bfloat16),
            pltpu.VMEM((3 * BAND, D), jnp.bfloat16),
            pltpu.VMEM((3 * BAND, D), jnp.bfloat16),
            pltpu.SemaphoreType.DMA((32,)),
        ],
        compiler_params=pltpu.CompilerParams(vmem_limit_bytes=48 * 1024 * 1024),
        cost_estimate=pl.CostEstimate(
            flops=12_000_000_000, bytes_accessed=20_000_000, transcendentals=2_000_000
        ),
        name="two_steps",
    )(
        place,
        normed,
        window,
        bias_first,
        gate_first,
        mod_second,
        bias_second,
        gain_query[None, :],
        gain_key[None, :],
        own,
        own_across,
        far,
        far_across,
    )


def solution(mesh):
    inner = Mesh(mesh.devices.reshape(SHAPE), AXES)
    queue_dp = P(AXES, None)
    dp = P(("y", "zh"), None)
    in_specs = (queue_dp, dp, P(), queue_dp, P(), dp, dp, dp, P(), P())
    return jax.shard_map(shards, mesh=inner, in_specs=in_specs, out_specs=queue_dp, check_vma=False)
```

```python
import jax
import jax.numpy as jnp
from jax import lax
from jax.experimental import pallas as pl
from jax.experimental.pallas import tpu as pltpu
from jax.sharding import Mesh, PartitionSpec as P

HEADS = 12
HEAD_DIM = 128
D = HEADS * HEAD_DIM
BAND = 112
PER_SECTION = 16
SECTIONS = 32
DEVICES = SECTIONS * PER_SECTION
LEVELS = 32
ROWS = D // PER_SECTION
HALF = 3 * D // 2
TILE = 768
FLAGS = 16
EPSILON = 1e-06
SHAPE = (4, 4, 2, 8, 2)
AXES = ("zl", "x", "core", "y", "zh")
SCALE = HEAD_DIM**-0.5 * 1.4426950408889634


def layer_norm(values):
    average = jnp.mean(values, axis=-1, keepdims=True)
    centred = values - average
    spread = jnp.mean(centred * centred, axis=-1, keepdims=True)
    return centred * lax.rsqrt(spread + EPSILON)


def level_of(levels, step, band):
    section = lax.div(jnp.clip(band, 0, DEVICES - 1), jnp.int32(PER_SECTION))
    return levels[step, section]


def mod_row(mod_ref, part, level):
    return mod_ref[pl.ds(part * LEVELS + level, 1), :]


def modulated(values, mod_ref, level):
    normed = layer_norm(values.astype(jnp.float32))
    return (normed * (1.0 + mod_row(mod_ref, 1, level)) + mod_row(mod_ref, 0, level)).astype(jnp.bfloat16)


def prepare(place, levels, mod_ref, *rest):
    out_ref = rest[-1]
    for i in range(5):
        level = level_of(levels, 0, place[0] - PER_SECTION + i - 2)
        out_ref[i * BAND : (i + 1) * BAND, :] = modulated(rest[i][:BAND, :], mod_ref, level)


def attend(query, key, value, first, bias):
    scores = lax.dot_general(
        query[first : first + BAND],
        key[first : first + 3 * BAND],
        (((1,), (1,)), ((), ())),
        preferred_element_type=jnp.float32,
    )
    scores = scores + bias
    peak = jnp.max(scores, axis=-1, keepdims=True)
    weights = jnp.exp2(scores - peak).astype(jnp.bfloat16)
    mixed = jnp.dot(weights, value[first : first + 3 * BAND], preferred_element_type=jnp.float32)
    return (mixed[:, :HEAD_DIM] / mixed[:, HEAD_DIM:]).astype(jnp.bfloat16)


def bias_row(previous, following):
    lane = lax.broadcasted_iota(jnp.int32, (1, 3 * BAND), 1)
    closed = jnp.where(lane < BAND, previous, jnp.where(lane >= 2 * BAND, following, 0.0))
    return closed * -1e30


def compute(
    place,
    levels,
    bounds,
    mod_ref,
    normed_ref,
    before_ref,
    middle_ref,
    after_ref,
    gain_query_ref,
    gain_key_ref,
    gathered_ref,
    out_ref,
    weights,
    query,
    key,
    value,
    advanced,
    normed,
    gates,
    sem,
):
    frame = place[0]
    windows = (before_ref, middle_ref, after_ref)

    def copy_of(tile, y):
        core, first = divmod(tile * TILE, HALF)
        block = (2 * y + core) * 2 * ROWS
        return pltpu.make_async_copy(
            gathered_ref.at[pl.ds(block, 2 * ROWS), pl.ds(first, TILE)],
            weights.at[pl.ds(y * 2 * ROWS, 2 * ROWS), pl.ds(tile * TILE, TILE)],
            sem.at[tile * 8 + y],
        )

    for tile in range(6):
        for y in range(8):
            copy_of(tile, y).start()

    def arrived(tile):
        for y in range(8):
            copy_of(tile, y).wait()

    def project(source, bands, first_use):
        rows = bands * BAND
        inner = (bands - 2) * BAND

        def tile(index, rows_of):
            return jnp.dot(
                source[rows_of, :],
                weights[:, index * TILE : (index + 1) * TILE],
                preferred_element_type=jnp.float32,
            )

        def folded(product):
            squares = product * product
            return sum(squares[:, i : i + 128] for i in range(0, TILE, 128))

        def norm(power):
            return lax.rsqrt(jnp.sum(power, axis=-1, keepdims=True) * (1.0 / D) + EPSILON)

        query_power = key_power = 0.0
        for i in range(2):
            if first_use:
                arrived(i)
            product = tile(i, slice(BAND, BAND + inner))
            query[:inner, i * TILE : (i + 1) * TILE] = product
            query_power = query_power + folded(product)
        for i in range(2):
            if first_use:
                arrived(2 + i)
            product = tile(2 + i, slice(0, rows))
            key[:rows, i * TILE : (i + 1) * TILE] = product
            key_power = key_power + folded(product)
        for i in range(2):
            if first_use:
                arrived(4 + i)
            value[:rows, i * TILE : (i + 1) * TILE] = tile(4 + i, slice(0, rows)).astype(jnp.bfloat16)
        return norm(query_power), norm(key_power)

    def heads_of(bands, query_norm, key_norm, biases, finish):
        rows = bands * BAND
        inner = (bands - 2) * BAND

        def one_head(h, carry):
            lanes = pl.ds(pl.multiple_of(h * HEAD_DIM, HEAD_DIM), HEAD_DIM)
            head_query = (query[:inner, lanes] * query_norm * (gain_query_ref[:, lanes] * SCALE)).astype(jnp.bfloat16)
            head_key = (key[:rows, lanes] * key_norm * gain_key_ref[:, lanes]).astype(jnp.bfloat16)
            head_value = jnp.concatenate(
                [value[:rows, lanes], jnp.ones((rows, HEAD_DIM), jnp.bfloat16)], axis=1
            )
            for band in range(bands - 2):
                attended = attend(head_query, head_key, head_value, band * BAND, biases[band])
                finish(band, lanes, attended.astype(jnp.float32))
            return carry

        lax.fori_loop(0, HEADS, one_head, 0, unroll=4)

    query_norm, key_norm = project(normed_ref, 5, True)

    biases = []
    for window in windows:
        flags = window[BAND : BAND + FLAGS, : 3 * BAND].astype(jnp.float32)
        biases.append(bias_row(flags[0:1], flags[1:2]))

    for band in range(3):
        gates[band : band + 1, :] = mod_row(mod_ref, 2, level_of(levels, 0, frame - PER_SECTION + band - 1))
    gates[3:4, :] = mod_row(mod_ref, 2, level_of(levels, 1, frame))

    def finish_first(band, lanes, attended):
        gate = gates[band : band + 1, lanes]
        held = windows[band][:BAND, lanes]
        moved = (held.astype(jnp.float32) + gate * attended).astype(jnp.bfloat16)
        entering = jnp.where(frame + band - 1 < PER_SECTION, held, moved)
        advanced[band * BAND : (band + 1) * BAND, lanes] = entering

    heads_of(5, query_norm, key_norm, biases, finish_first)

    for band in range(3):
        rows = slice(band * BAND, (band + 1) * BAND)
        normed[rows, :] = modulated(advanced[rows, :], mod_ref, level_of(levels, 1, frame + band - 1))

    query_norm, key_norm = project(normed, 3, False)

    bias_second = bias_row(
        jnp.where(bounds[0, 0] >= frame, 1.0, 0.0), jnp.where(bounds[0, 1] <= frame + 1, 1.0, 0.0)
    )

    def finish_second(band, lanes, attended):
        gate = gates[3:4, lanes]
        held = advanced[BAND : 2 * BAND, lanes].astype(jnp.float32)
        out_ref[:, lanes] = (held + gate * attended).astype(jnp.bfloat16)

    heads_of(3, query_norm, key_norm, [bias_second], finish_second)


def prepared(place, levels, table, bands):
    smem = pl.BlockSpec(memory_space=pltpu.SMEM)
    vmem = pl.BlockSpec(memory_space=pltpu.VMEM)
    return pl.pallas_call(
        prepare,
        out_shape=jax.ShapeDtypeStruct((5 * BAND, D), jnp.bfloat16),
        in_specs=[smem] * 2 + [vmem] * 6,
        out_specs=vmem,
        compiler_params=pltpu.CompilerParams(vmem_limit_bytes=16 * 1024 * 1024),
        cost_estimate=pl.CostEstimate(flops=10_000_000, bytes_accessed=4_000_000, transcendentals=0),
        name="normed_window",
    )(place, levels, table, *bands)


def two_steps(place, levels, bounds, table, normed, windows, gain_query, gain_key, gathered):
    smem = pl.BlockSpec(memory_space=pltpu.SMEM)
    vmem = pl.BlockSpec(memory_space=pltpu.VMEM)
    anywhere = pl.BlockSpec(memory_space=pl.ANY)
    return pl.pallas_call(
        compute,
        out_shape=jax.ShapeDtypeStruct((BAND, D), jnp.bfloat16),
        in_specs=[smem] * 3 + [vmem] * 7 + [anywhere],
        out_specs=vmem,
        scratch_shapes=[
            pltpu.VMEM((D, 3 * D), jnp.bfloat16),
            pltpu.VMEM((3 * BAND, D), jnp.float32),
            pltpu.VMEM((5 * BAND, D), jnp.float32),
            pltpu.VMEM((5 * BAND, D), jnp.bfloat16),
            pltpu.VMEM((3 * BAND, D), jnp.bfloat16),
            pltpu.VMEM((3 * BAND, D), jnp.bfloat16),
            pltpu.VMEM((8, D), jnp.float32),
            pltpu.SemaphoreType.DMA((48,)),
        ],
        compiler_params=pltpu.CompilerParams(vmem_limit_bytes=48 * 1024 * 1024),
        cost_estimate=pl.CostEstimate(
            flops=12_000_000_000, bytes_accessed=20_000_000, transcendentals=2_000_000
        ),
        name="two_steps",
    )(place, levels, bounds, table, normed, *windows, gain_query, gain_key, gathered)


def tied(value, *others):
    return lax.optimization_barrier((value, *others))[0]


def shards(
    stream, incoming, levels, bounds, mod_table, w_query, w_key, w_value, gain_query, gain_key
):
    core = lax.axis_index("core")
    frame = lax.axis_index(AXES)
    zh = lax.axis_index("zh")
    place = frame.astype(jnp.int32)[None]

    half = jnp.where(
        core == 0,
        jnp.concatenate([w_query, w_key[:, : HALF - D]], axis=1),
        jnp.concatenate([w_key[:, HALF - D :], w_value], axis=1),
    )
    opposite = lax.ppermute(half, "zh", [(0, 1), (1, 0)])
    both = jnp.where(
        zh == 0, jnp.concatenate([half, opposite], axis=0), jnp.concatenate([opposite, half], axis=0)
    )
    gathered = lax.all_gather(both, ("y", "core"), axis=0, tiled=True)

    row = lax.broadcasted_iota(jnp.int32, (FLAGS, D), 0)
    flags = jnp.where(row == 0, bounds[0, 0] >= frame, bounds[0, 1] <= frame + 1).astype(jnp.bfloat16)
    last = frame >= DEVICES - PER_SECTION
    payloads = {
        -2: stream,
        -1: jnp.concatenate([jnp.where(last, incoming, stream), flags], axis=0),
        1: jnp.concatenate([jnp.where(frame > DEVICES - PER_SECTION, incoming, stream), flags], axis=0),
        2: stream,
    }
    payloads[0] = payloads[-1]
    bands = {}
    for k in range(-2, 3):
        route = [(d, (d + PER_SECTION - k) % DEVICES) for d in range(DEVICES)]
        bands[k] = lax.ppermute(tied(payloads[k], opposite), AXES, route)

    table = mod_table.transpose(1, 0, 2).reshape(3 * LEVELS, D)
    normed = prepared(place, levels, table, [bands[k] for k in range(-2, 3)])
    return two_steps(
        place,
        levels,
        bounds,
        table,
        normed,
        [bands[k] for k in (-1, 0, 1)],
        gain_query[None, :],
        gain_key[None, :],
        gathered,
    )


def solution(mesh):
    inner = Mesh(mesh.devices.reshape(SHAPE), AXES)
    queue_dp = P(AXES, None)
    dp = P(("y", "zh"), None)
    in_specs = (queue_dp, dp, P(), queue_dp, P(), dp, dp, dp, P(), P())
    return jax.shard_map(shards, mesh=inner, in_specs=in_specs, out_specs=queue_dp, check_vma=False)
```

```python
import jax
import jax.numpy as jnp
from jax import lax
from jax.experimental import pallas as pl
from jax.experimental.pallas import tpu as pltpu
from jax.sharding import Mesh, PartitionSpec as P

HEADS = 12
HEAD_DIM = 128
D = HEADS * HEAD_DIM
BAND = 112
PER_SECTION = 16
SECTIONS = 32
DEVICES = SECTIONS * PER_SECTION
LEVELS = 32
ROWS = D // PER_SECTION
HALF = 3 * D // 2
COPY = 768
TILES = ((0, 768), (768, 1536), (1536, 2304), (2304, 3072), (3072, 4608))
FLAGS = 16
HELD = BAND + FLAGS
EPSILON = 1e-06
SHAPE = (4, 4, 2, 8, 2)
AXES = ("zl", "x", "core", "y", "zh")
SCALE = HEAD_DIM**-0.5 * 1.4426950408889634


def layer_norm(values):
    average = jnp.mean(values, axis=-1, keepdims=True)
    centred = values - average
    spread = jnp.mean(centred * centred, axis=-1, keepdims=True)
    return centred * lax.rsqrt(spread + EPSILON)


def level_of(levels, step, band):
    section = lax.div(jnp.clip(band, 0, DEVICES - 1), jnp.int32(PER_SECTION))
    return levels[step, section]


def mod_row(mod_ref, part, level):
    return mod_ref[pl.ds(part * LEVELS + level, 1), :]


def modulated(values, mod_ref, level):
    normed = layer_norm(values.astype(jnp.float32))
    return (normed * (1.0 + mod_row(mod_ref, 1, level)) + mod_row(mod_ref, 0, level)).astype(jnp.bfloat16)


def prepare(place, levels, mod_ref, around_ref, out_ref, window_ref):
    start = 2 * BAND
    middle = around_ref[start : start + HELD, :]
    partner = around_ref[start + HELD : start + 2 * HELD, :]
    diagonal = around_ref[start + 2 * HELD : start + 3 * HELD, :]
    even = place[1] == 0
    bands = [
        around_ref[:BAND, :],
        jnp.where(even, diagonal, partner),
        middle,
        jnp.where(even, partner, diagonal),
        around_ref[BAND : 2 * BAND, :],
    ]
    for i, band in enumerate(bands):
        level = level_of(levels, 0, place[0] - PER_SECTION + i - 2)
        out_ref[i * BAND : (i + 1) * BAND, :] = modulated(band[:BAND], mod_ref, level)
        if 0 < i < 4:
            window_ref[(i - 1) * HELD : i * HELD, :] = band


def attend(query, key, value, first, bias):
    scores = lax.dot_general(
        query[first : first + BAND],
        key[first : first + 3 * BAND],
        (((1,), (1,)), ((), ())),
        preferred_element_type=jnp.float32,
    )
    scores = scores + bias
    peak = jnp.max(scores, axis=-1, keepdims=True)
    weights = jnp.exp2(scores - peak).astype(jnp.bfloat16)
    mixed = jnp.dot(weights, value[first : first + 3 * BAND], preferred_element_type=jnp.float32)
    return (mixed[:, :HEAD_DIM] / mixed[:, HEAD_DIM:]).astype(jnp.bfloat16)


def bias_row(previous, following):
    lane = lax.broadcasted_iota(jnp.int32, (1, 3 * BAND), 1)
    closed = jnp.where(lane < BAND, previous, jnp.where(lane >= 2 * BAND, following, 0.0))
    return closed * -1e30


def compute(
    place,
    levels,
    bounds,
    mod_ref,
    normed_ref,
    window_ref,
    gain_query_ref,
    gain_key_ref,
    gathered_ref,
    out_ref,
    weights,
    query,
    key,
    value,
    advanced,
    normed,
    gates,
    sem,
):
    frame = place[0]

    def copy_of(tile):
        core, first = divmod(tile * COPY, HALF)
        return pltpu.make_async_copy(
            gathered_ref.at[:, core, :, pl.ds(first, COPY)],
            weights.at[:, :, pl.ds(tile * COPY, COPY)],
            sem.at[tile],
        )

    for tile in range(6):
        copy_of(tile).start()

    def project(source, bands, first_use):
        rows = bands * BAND
        inner = (bands - 2) * BAND

        def folded(product):
            squares = product * product
            return sum(squares[:, i : i + 128] for i in range(0, squares.shape[1], 128))

        def norm(power):
            return lax.rsqrt(jnp.sum(power, axis=-1, keepdims=True) * (1.0 / D) + EPSILON)

        query_power = key_power = 0.0
        for first, end in TILES:
            if first_use:
                for i in range(first // COPY, end // COPY):
                    copy_of(i).wait()
            spot = slice(first % D, (end - 1) % D + 1)
            tile = weights[:, :, first:end].reshape(D, end - first)
            used = source[BAND : BAND + inner, :] if end <= D else source[:rows, :]
            product = jnp.dot(used, tile, preferred_element_type=jnp.float32)
            if end <= D:
                query[:inner, spot] = product
                query_power = query_power + folded(product)
            elif end <= 2 * D:
                key[:rows, spot] = product
                key_power = key_power + folded(product)
            else:
                value[:rows, spot] = product.astype(jnp.bfloat16)
        return norm(query_power), norm(key_power)

    def heads_of(bands, query_norm, key_norm, biases, finish):
        rows = bands * BAND
        inner = (bands - 2) * BAND

        def one_head(h, carry):
            lanes = pl.ds(pl.multiple_of(h * HEAD_DIM, HEAD_DIM), HEAD_DIM)
            head_query = (query[:inner, lanes] * query_norm * (gain_query_ref[:, lanes] * SCALE)).astype(jnp.bfloat16)
            head_key = (key[:rows, lanes] * key_norm * gain_key_ref[:, lanes]).astype(jnp.bfloat16)
            head_value = jnp.concatenate(
                [value[:rows, lanes], jnp.ones((rows, HEAD_DIM), jnp.bfloat16)], axis=1
            )
            for band in range(bands - 2):
                attended = attend(head_query, head_key, head_value, band * BAND, biases[band])
                finish(band, lanes, attended.astype(jnp.float32))
            return carry

        lax.fori_loop(0, HEADS, one_head, 0, unroll=HEADS)

    query_norm, key_norm = project(normed_ref, 5, True)

    biases = []
    for band in range(3):
        flags = window_ref[band * HELD + BAND : (band + 1) * HELD, : 3 * BAND].astype(jnp.float32)
        biases.append(bias_row(flags[0:1], flags[1:2]))

    for band in range(3):
        gates[band : band + 1, :] = mod_row(mod_ref, 2, level_of(levels, 0, frame - PER_SECTION + band - 1))
    gates[3:4, :] = mod_row(mod_ref, 2, level_of(levels, 1, frame))

    def finish_first(band, lanes, attended):
        gate = gates[band : band + 1, lanes]
        held = window_ref[band * HELD : band * HELD + BAND, lanes]
        moved = (held.astype(jnp.float32) + gate * attended).astype(jnp.bfloat16)
        entering = jnp.where(frame + band - 1 < PER_SECTION, held, moved)
        advanced[band * BAND : (band + 1) * BAND, lanes] = entering

    heads_of(5, query_norm, key_norm, biases, finish_first)

    for band in range(3):
        rows = slice(band * BAND, (band + 1) * BAND)
        normed[rows, :] = modulated(advanced[rows, :], mod_ref, level_of(levels, 1, frame + band - 1))

    query_norm, key_norm = project(normed, 3, False)

    bias_second = bias_row(
        jnp.where(bounds[0, 0] >= frame, 1.0, 0.0), jnp.where(bounds[0, 1] <= frame + 1, 1.0, 0.0)
    )

    def finish_second(band, lanes, attended):
        gate = gates[3:4, lanes]
        held = advanced[BAND : 2 * BAND, lanes].astype(jnp.float32)
        out_ref[:, lanes] = (held + gate * attended).astype(jnp.bfloat16)

    heads_of(3, query_norm, key_norm, [bias_second], finish_second)


def prepared(place, levels, table, around):
    smem = pl.BlockSpec(memory_space=pltpu.SMEM)
    vmem = pl.BlockSpec(memory_space=pltpu.VMEM)
    return pl.pallas_call(
        prepare,
        out_shape=[
            jax.ShapeDtypeStruct((5 * BAND, D), jnp.bfloat16),
            jax.ShapeDtypeStruct((3 * HELD, D), jnp.bfloat16),
        ],
        in_specs=[smem] * 2 + [vmem] * 2,
        out_specs=[vmem] * 2,
        compiler_params=pltpu.CompilerParams(vmem_limit_bytes=16 * 1024 * 1024),
        cost_estimate=pl.CostEstimate(flops=10_000_000, bytes_accessed=4_000_000, transcendentals=0),
        name="normed_window",
    )(place, levels, table, around)


def two_steps(place, levels, bounds, table, normed, window, gain_query, gain_key, gathered):
    smem = pl.BlockSpec(memory_space=pltpu.SMEM)
    vmem = pl.BlockSpec(memory_space=pltpu.VMEM)
    anywhere = pl.BlockSpec(memory_space=pl.ANY)
    return pl.pallas_call(
        compute,
        out_shape=jax.ShapeDtypeStruct((BAND, D), jnp.bfloat16),
        in_specs=[smem] * 3 + [vmem] * 5 + [anywhere],
        out_specs=vmem,
        scratch_shapes=[
            pltpu.VMEM((8, 2 * ROWS, 3 * D), jnp.bfloat16),
            pltpu.VMEM((3 * BAND, D), jnp.float32),
            pltpu.VMEM((5 * BAND, D), jnp.float32),
            pltpu.VMEM((5 * BAND, D), jnp.bfloat16),
            pltpu.VMEM((3 * BAND, D), jnp.bfloat16),
            pltpu.VMEM((3 * BAND, D), jnp.bfloat16),
            pltpu.VMEM((8, D), jnp.float32),
            pltpu.SemaphoreType.DMA((6,)),
        ],
        compiler_params=pltpu.CompilerParams(vmem_limit_bytes=48 * 1024 * 1024),
        cost_estimate=pl.CostEstimate(
            flops=12_000_000_000, bytes_accessed=20_000_000, transcendentals=2_000_000
        ),
        name="two_steps",
    )(place, levels, bounds, table, normed, window, gain_query, gain_key, gathered)


def tied(value, *others):
    return lax.optimization_barrier((value, *others))[0]


def shards(
    stream, incoming, levels, bounds, mod_table, w_query, w_key, w_value, gain_query, gain_key
):
    core = lax.axis_index("core")
    frame = lax.axis_index(AXES)
    zh = lax.axis_index("zh")
    place = jnp.stack([frame, zh]).astype(jnp.int32)

    parity = lax.rem(lax.axis_index("x"), 2)
    packed = jnp.concatenate([w_query, w_key, w_value], axis=1)
    half = lax.dynamic_slice_in_dim(packed, core * HALF, HALF, axis=1)
    quarter = lax.dynamic_slice_in_dim(packed, core * HALF + parity * (HALF // 2), HALF // 2, axis=1)
    mirror = [(2 * zl + side, 2 * (3 - zl) + 1 - side) for zl in range(4) for side in range(2)]
    opposite = lax.ppermute(quarter, ("zl", "zh"), mirror)
    ring = [(i, (i + 1) % 4) for i in range(4)]
    beside = [(2 * i, 2 * j) for i, j in ring] + [(2 * j + 1, 2 * i + 1) for i, j in ring]
    neighbour = lax.ppermute(opposite, ("x", "core"), beside)
    row = lax.broadcasted_iota(jnp.int32, (FLAGS, D), 0)
    flags = jnp.where(row == 0, bounds[0, 0] >= frame, bounds[0, 1] <= frame + 1).astype(jnp.bfloat16)
    y = lax.axis_index("y")
    last = frame >= DEVICES - PER_SECTION
    mine = jnp.where(last, incoming, stream)
    flagged = lambda block: jnp.concatenate([block, flags], axis=0)
    held = flagged(mine)

    def moved(block, distance):
        route = [(d, (d + distance) % DEVICES) for d in range(DEVICES)]
        return lax.ppermute(block, AXES, route)

    two_before = moved(mine, 2)
    two_after = moved(jnp.where(last & (y > 0), incoming, stream), -2)
    neighbour = tied(neighbour, two_before, two_after)
    other = jnp.where(
        parity == 0,
        jnp.concatenate([opposite, neighbour], axis=1),
        jnp.concatenate([neighbour, opposite], axis=1),
    )
    both = jnp.where(
        zh == 0, jnp.concatenate([half, other], axis=0), jnp.concatenate([other, half], axis=0)
    )
    gathered = lax.all_gather(both, ("y", "core"), axis=0, tiled=True)

    partner = lax.ppermute(tied(held, opposite), "zh", [(0, 1), (1, 0)])
    diagonal = lax.ppermute(
        tied(flagged(jnp.where(last & (y + zh > 0), incoming, stream)), opposite),
        AXES,
        [(d, (d + 1 if d % 2 else d - 1) % DEVICES) for d in range(DEVICES)],
    )
    around = moved(jnp.concatenate([two_before, two_after, held, partner, diagonal], axis=0), PER_SECTION)

    table = mod_table.transpose(1, 0, 2).reshape(3 * LEVELS, D)
    normed, window = prepared(place, levels, table, around)
    return two_steps(
        place,
        levels,
        bounds,
        table,
        normed,
        window,
        gain_query[None, :],
        gain_key[None, :],
        gathered.reshape(8, 2, 2 * ROWS, HALF),
    )


def solution(mesh):
    inner = Mesh(mesh.devices.reshape(SHAPE), AXES)
    queue_dp = P(AXES, None)
    dp = P(("y", "zh"), None)
    in_specs = (queue_dp, dp, P(), queue_dp, P(), dp, dp, dp, P(), P())
    return jax.shard_map(shards, mesh=inner, in_specs=in_specs, out_specs=queue_dp, check_vma=False)
```

```python
import jax
import jax.numpy as jnp
from jax import lax
from jax.experimental import pallas as pl
from jax.experimental.pallas import tpu as pltpu
from jax.sharding import Mesh, PartitionSpec as P

HEADS = 12
HEAD_DIM = 128
D = HEADS * HEAD_DIM
BAND = 112
PER_SECTION = 16
SECTIONS = 32
DEVICES = SECTIONS * PER_SECTION
LEVELS = 32
ROWS = D // PER_SECTION
HALF = 3 * D // 2
COPY = 768
TILES = ((0, 768), (768, 1536), (1536, 3072), (3072, 4608))
FLAGS = 16
HELD = BAND + FLAGS
EPSILON = 1e-06
SHAPE = (4, 4, 2, 8, 2)
AXES = ("zl", "x", "core", "y", "zh")
SCALE = HEAD_DIM**-0.5 * 1.4426950408889634


def layer_norm(values):
    average = jnp.mean(values, axis=-1, keepdims=True)
    centred = values - average
    spread = jnp.mean(centred * centred, axis=-1, keepdims=True)
    return centred * lax.rsqrt(spread + EPSILON)


def level_of(levels, step, band):
    section = lax.div(jnp.clip(band, 0, DEVICES - 1), jnp.int32(PER_SECTION))
    return levels[step, section]


def mod_row(mod_ref, part, level):
    return mod_ref[pl.ds(part * LEVELS + level, 1), :]


def modulated(values, mod_ref, level):
    normed = layer_norm(values.astype(jnp.float32))
    return (normed * (1.0 + mod_row(mod_ref, 1, level)) + mod_row(mod_ref, 0, level)).astype(jnp.bfloat16)


def prepare(place, levels, mod_ref, around_ref, out_ref, window_ref):
    start = 2 * HELD
    middle = around_ref[start : start + HELD, :]
    partner = around_ref[start + HELD : start + 2 * HELD, :]
    diagonal = around_ref[start + 2 * HELD : start + 3 * HELD, :]
    even = place[1] == 0
    bands = [
        around_ref[:HELD, :],
        jnp.where(even, diagonal, partner),
        middle,
        jnp.where(even, partner, diagonal),
        around_ref[HELD : 2 * HELD, :],
    ]
    for i, band in enumerate(bands):
        level = level_of(levels, 0, place[0] - PER_SECTION + i - 2)
        out_ref[i * BAND : (i + 1) * BAND, :] = modulated(band[:BAND], mod_ref, level)
        if 0 < i < 4:
            window_ref[(i - 1) * HELD : i * HELD, :] = band


def attend(query, key, value, first, bias):
    scores = lax.dot_general(
        query[first : first + BAND],
        key[first : first + 3 * BAND],
        (((1,), (1,)), ((), ())),
        preferred_element_type=jnp.float32,
    )
    scores = scores + bias
    peak = jnp.max(scores, axis=-1, keepdims=True)
    weights = jnp.exp2(scores - peak).astype(jnp.bfloat16)
    mixed = jnp.dot(weights, value[first : first + 3 * BAND], preferred_element_type=jnp.float32)
    return (mixed[:, :HEAD_DIM] / mixed[:, HEAD_DIM:]).astype(jnp.bfloat16)


def bias_row(previous, following):
    lane = lax.broadcasted_iota(jnp.int32, (1, 3 * BAND), 1)
    closed = jnp.where(lane < BAND, previous, jnp.where(lane >= 2 * BAND, following, 0.0))
    return closed * -1e30


def compute(
    place,
    levels,
    bounds,
    mod_ref,
    normed_ref,
    window_ref,
    gain_query_ref,
    gain_key_ref,
    gathered_ref,
    out_ref,
    weights,
    query,
    key,
    value,
    advanced,
    normed,
    gates,
    sem,
):
    frame = place[0]

    def copy_of(tile):
        core, first = divmod(tile * COPY, HALF)
        return pltpu.make_async_copy(
            gathered_ref.at[:, core, :, pl.ds(first, COPY)],
            weights.at[:, :, pl.ds(tile * COPY, COPY)],
            sem.at[tile],
        )

    for tile in range(6):
        copy_of(tile).start()

    def project(source, bands, first_use):
        rows = bands * BAND
        inner = (bands - 2) * BAND

        def folded(product):
            squares = product * product
            return sum(squares[:, i : i + 128] for i in range(0, squares.shape[1], 128))

        def norm(power):
            return lax.rsqrt(jnp.sum(power, axis=-1, keepdims=True) * (1.0 / D) + EPSILON)

        query_power = key_power = 0.0
        for first, end in TILES:
            if first_use:
                for i in range(first // COPY, end // COPY):
                    copy_of(i).wait()
            spot = slice(first % D, (end - 1) % D + 1)
            tile = weights[:, :, first:end].reshape(D, end - first)
            used = source[BAND : BAND + inner, :] if end <= D else source[:rows, :]
            product = jnp.dot(used, tile, preferred_element_type=jnp.float32)
            if end <= D:
                query[:inner, spot] = product
                query_power = query_power + folded(product)
            elif end <= 2 * D:
                key[:rows, spot] = product
                key_power = key_power + folded(product)
            else:
                value[:rows, spot] = product.astype(jnp.bfloat16)
        return norm(query_power), norm(key_power)

    def heads_of(bands, query_norm, key_norm, biases, finish):
        rows = bands * BAND
        inner = (bands - 2) * BAND

        def one_head(h, carry):
            lanes = pl.ds(pl.multiple_of(h * HEAD_DIM, HEAD_DIM), HEAD_DIM)
            head_query = (query[:inner, lanes] * query_norm * (gain_query_ref[:, lanes] * SCALE)).astype(jnp.bfloat16)
            head_key = (key[:rows, lanes] * key_norm * gain_key_ref[:, lanes]).astype(jnp.bfloat16)
            head_value = jnp.concatenate(
                [value[:rows, lanes], jnp.ones((rows, HEAD_DIM), jnp.bfloat16)], axis=1
            )
            for band in range(bands - 2):
                attended = attend(head_query, head_key, head_value, band * BAND, biases[band])
                finish(band, lanes, attended.astype(jnp.float32))
            return carry

        lax.fori_loop(0, HEADS, one_head, 0, unroll=HEADS)

    query_norm, key_norm = project(normed_ref, 5, True)

    biases = []
    for band in range(3):
        flags = window_ref[band * HELD + BAND : (band + 1) * HELD, : 3 * BAND].astype(jnp.float32)
        biases.append(bias_row(flags[0:1], flags[1:2]))

    for band in range(3):
        gates[band : band + 1, :] = mod_row(mod_ref, 2, level_of(levels, 0, frame - PER_SECTION + band - 1))
    gates[3:4, :] = mod_row(mod_ref, 2, level_of(levels, 1, frame))

    def finish_first(band, lanes, attended):
        gate = gates[band : band + 1, lanes]
        held = window_ref[band * HELD : band * HELD + BAND, lanes]
        moved = (held.astype(jnp.float32) + gate * attended).astype(jnp.bfloat16)
        entering = jnp.where(frame + band - 1 < PER_SECTION, held, moved)
        advanced[band * BAND : (band + 1) * BAND, lanes] = entering

    heads_of(5, query_norm, key_norm, biases, finish_first)

    for band in range(3):
        rows = slice(band * BAND, (band + 1) * BAND)
        normed[rows, :] = modulated(advanced[rows, :], mod_ref, level_of(levels, 1, frame + band - 1))

    query_norm, key_norm = project(normed, 3, False)

    bias_second = bias_row(
        jnp.where(bounds[0, 0] >= frame, 1.0, 0.0), jnp.where(bounds[0, 1] <= frame + 1, 1.0, 0.0)
    )

    def finish_second(band, lanes, attended):
        gate = gates[3:4, lanes]
        held = advanced[BAND : 2 * BAND, lanes].astype(jnp.float32)
        out_ref[:, lanes] = (held + gate * attended).astype(jnp.bfloat16)

    heads_of(3, query_norm, key_norm, [bias_second], finish_second)


def prepared(place, levels, table, around):
    smem = pl.BlockSpec(memory_space=pltpu.SMEM)
    vmem = pl.BlockSpec(memory_space=pltpu.VMEM)
    return pl.pallas_call(
        prepare,
        out_shape=[
            jax.ShapeDtypeStruct((5 * BAND, D), jnp.bfloat16),
            jax.ShapeDtypeStruct((3 * HELD, D), jnp.bfloat16),
        ],
        in_specs=[smem] * 2 + [vmem] * 2,
        out_specs=[vmem] * 2,
        compiler_params=pltpu.CompilerParams(vmem_limit_bytes=16 * 1024 * 1024),
        cost_estimate=pl.CostEstimate(flops=10_000_000, bytes_accessed=4_000_000, transcendentals=0),
        name="normed_window",
    )(place, levels, table, around)


def two_steps(place, levels, bounds, table, normed, window, gain_query, gain_key, gathered):
    smem = pl.BlockSpec(memory_space=pltpu.SMEM)
    vmem = pl.BlockSpec(memory_space=pltpu.VMEM)
    anywhere = pl.BlockSpec(memory_space=pl.ANY)
    return pl.pallas_call(
        compute,
        out_shape=jax.ShapeDtypeStruct((BAND, D), jnp.bfloat16),
        in_specs=[smem] * 3 + [vmem] * 5 + [anywhere],
        out_specs=vmem,
        scratch_shapes=[
            pltpu.VMEM((8, 2 * ROWS, 3 * D), jnp.bfloat16),
            pltpu.VMEM((3 * BAND, D), jnp.float32),
            pltpu.VMEM((5 * BAND, D), jnp.float32),
            pltpu.VMEM((5 * BAND, D), jnp.bfloat16),
            pltpu.VMEM((3 * BAND, D), jnp.bfloat16),
            pltpu.VMEM((3 * BAND, D), jnp.bfloat16),
            pltpu.VMEM((8, D), jnp.float32),
            pltpu.SemaphoreType.DMA((6,)),
        ],
        compiler_params=pltpu.CompilerParams(vmem_limit_bytes=48 * 1024 * 1024),
        cost_estimate=pl.CostEstimate(
            flops=12_000_000_000, bytes_accessed=20_000_000, transcendentals=2_000_000
        ),
        name="two_steps",
    )(place, levels, bounds, table, normed, window, gain_query, gain_key, gathered)


def tied(value, *others):
    return lax.optimization_barrier((value, *others))[0]


def shards(
    stream, incoming, levels, bounds, mod_table, w_query, w_key, w_value, gain_query, gain_key
):
    core = lax.axis_index("core")
    frame = lax.axis_index(AXES)
    zh = lax.axis_index("zh")
    place = jnp.stack([frame, zh]).astype(jnp.int32)

    parity = lax.rem(lax.axis_index("x"), 2)
    packed = jnp.concatenate([w_query, w_key, w_value], axis=1)
    half = lax.dynamic_slice_in_dim(packed, core * HALF, HALF, axis=1)
    quarter = lax.dynamic_slice_in_dim(packed, core * HALF + parity * (HALF // 2), HALF // 2, axis=1)
    mirror = [(2 * zl + side, 2 * (3 - zl) + 1 - side) for zl in range(4) for side in range(2)]
    opposite = lax.ppermute(quarter, ("zl", "zh"), mirror)
    ring = [(i, (i + 1) % 4) for i in range(4)]
    beside = [(2 * i, 2 * j) for i, j in ring] + [(2 * j + 1, 2 * i + 1) for i, j in ring]
    neighbour = lax.ppermute(opposite, ("x", "core"), beside)
    row = lax.broadcasted_iota(jnp.int32, (FLAGS, D), 0)
    flags = jnp.where(row == 0, bounds[0, 0] >= frame, bounds[0, 1] <= frame + 1).astype(jnp.bfloat16)
    y = lax.axis_index("y")
    last = frame >= DEVICES - PER_SECTION
    mine = jnp.where(last, incoming, stream)
    flagged = lambda block: jnp.concatenate([block, flags], axis=0)
    held = flagged(mine)

    def moved(block, distance):
        route = [(d, (d + distance) % DEVICES) for d in range(DEVICES)]
        return lax.ppermute(block, AXES, route)

    two_before = moved(held, 2)
    two_after = moved(flagged(jnp.where(last & (y > 0), incoming, stream)), -2)
    neighbour = tied(neighbour, two_before, two_after)
    other = jnp.where(
        parity == 0,
        jnp.concatenate([opposite, neighbour], axis=1),
        jnp.concatenate([neighbour, opposite], axis=1),
    )
    both = jnp.where(
        zh == 0, jnp.concatenate([half, other], axis=0), jnp.concatenate([other, half], axis=0)
    )
    gathered = lax.all_gather(both, ("y", "core"), axis=0, tiled=True)

    given = jnp.concatenate([held, jnp.where(zh == 1, two_before, two_after)], axis=0)
    taken = lax.ppermute(tied(given, opposite), "zh", [(0, 1), (1, 0)])
    around = moved(jnp.concatenate([two_before, two_after, held, taken], axis=0), PER_SECTION)

    table = mod_table.transpose(1, 0, 2).reshape(3 * LEVELS, D)
    normed, window = prepared(place, levels, table, around)
    return two_steps(
        place,
        levels,
        bounds,
        table,
        normed,
        window,
        gain_query[None, :],
        gain_key[None, :],
        gathered.reshape(8, 2, 2 * ROWS, HALF),
    )


def solution(mesh):
    inner = Mesh(mesh.devices.reshape(SHAPE), AXES)
    queue_dp = P(AXES, None)
    dp = P(("y", "zh"), None)
    in_specs = (queue_dp, dp, P(), queue_dp, P(), dp, dp, dp, P(), P())
    return jax.shard_map(shards, mesh=inner, in_specs=in_specs, out_specs=queue_dp, check_vma=False)
```

```python
import jax
import jax.numpy as jnp
from jax import lax
from jax.experimental import pallas as pl
from jax.experimental.pallas import tpu as pltpu
from jax.sharding import Mesh, PartitionSpec as P

HEADS = 12
HEAD_DIM = 128
D = HEADS * HEAD_DIM
BAND = 112
PER_SECTION = 16
SECTIONS = 32
DEVICES = SECTIONS * PER_SECTION
LEVELS = 32
ROWS = D // PER_SECTION
HALF = 3 * D // 2
COPY = 768
TILES = ((0, 768), (768, 1536), (1536, 3072), (3072, 4608))
FLAGS = 16
HELD = BAND + FLAGS
EPSILON = 1e-06
SHAPE = (4, 4, 2, 8, 2)
AXES = ("zl", "x", "core", "y", "zh")
SCALE = HEAD_DIM**-0.5 * 1.4426950408889634


def layer_norm(values):
    average = jnp.mean(values, axis=-1, keepdims=True)
    centred = values - average
    spread = jnp.mean(centred * centred, axis=-1, keepdims=True)
    return centred * lax.rsqrt(spread + EPSILON)


def level_of(levels, step, band):
    section = lax.div(jnp.clip(band, 0, DEVICES - 1), jnp.int32(PER_SECTION))
    return levels[step, section]


def mod_row(mod_ref, part, level):
    return mod_ref[pl.ds(part * LEVELS + level, 1), :]


def modulated(values, mod_ref, level):
    normed = layer_norm(values.astype(jnp.float32))
    return (normed * (1.0 + mod_row(mod_ref, 1, level)) + mod_row(mod_ref, 0, level)).astype(jnp.bfloat16)


def prepare(place, levels, mod_ref, around_ref, out_ref, window_ref):
    start = 2 * HELD
    middle = around_ref[start : start + HELD, :]
    partner = around_ref[start + HELD : start + 2 * HELD, :]
    diagonal = around_ref[start + 2 * HELD : start + 3 * HELD, :]
    even = place[1] == 0
    bands = [
        around_ref[:HELD, :],
        jnp.where(even, diagonal, partner),
        middle,
        jnp.where(even, partner, diagonal),
        around_ref[HELD : 2 * HELD, :],
    ]
    for i, band in enumerate(bands):
        level = level_of(levels, 0, place[0] - PER_SECTION + i - 2)
        out_ref[i * BAND : (i + 1) * BAND, :] = modulated(band[:BAND], mod_ref, level)
        if 0 < i < 4:
            window_ref[(i - 1) * HELD : i * HELD, :] = band


def attend(query, key, value, first, bias):
    scores = lax.dot_general(
        query[first : first + BAND],
        key[first : first + 3 * BAND],
        (((1,), (1,)), ((), ())),
        preferred_element_type=jnp.float32,
    )
    scores = scores + bias
    peak = jnp.max(scores, axis=-1, keepdims=True)
    weights = jnp.exp2(scores - peak).astype(jnp.bfloat16)
    mixed = jnp.dot(weights, value[first : first + 3 * BAND], preferred_element_type=jnp.float32)
    return (mixed[:, :HEAD_DIM] / mixed[:, HEAD_DIM:]).astype(jnp.bfloat16)


def bias_row(previous, following):
    lane = lax.broadcasted_iota(jnp.int32, (1, 3 * BAND), 1)
    closed = jnp.where(lane < BAND, previous, jnp.where(lane >= 2 * BAND, following, 0.0))
    return closed * -1e30


def compute(
    place,
    levels,
    bounds,
    mod_ref,
    normed_ref,
    window_ref,
    gain_query_ref,
    gain_key_ref,
    gathered_ref,
    out_ref,
    weights,
    query,
    key,
    value,
    advanced,
    normed,
    gates,
    sem,
):
    frame = place[0]

    def copy_of(tile):
        core, first = divmod(tile * COPY, HALF)
        return pltpu.make_async_copy(
            gathered_ref.at[:, core, :, pl.ds(first, COPY)],
            weights.at[:, :, pl.ds(tile * COPY, COPY)],
            sem.at[tile],
        )

    for tile in range(6):
        copy_of(tile).start()

    def project(source, bands, first_use):
        rows = bands * BAND
        inner = (bands - 2) * BAND

        def folded(product):
            squares = product * product
            return sum(squares[:, i : i + 128] for i in range(0, squares.shape[1], 128))

        def norm(power):
            return lax.rsqrt(jnp.sum(power, axis=-1, keepdims=True) * (1.0 / D) + EPSILON)

        query_power = key_power = 0.0
        for first, end in TILES:
            if first_use:
                for i in range(first // COPY, end // COPY):
                    copy_of(i).wait()
            spot = slice(first % D, (end - 1) % D + 1)
            tile = weights[:, :, first:end].reshape(D, end - first)
            used = source[BAND : BAND + inner, :] if end <= D else source[:rows, :]
            product = jnp.dot(used, tile, preferred_element_type=jnp.float32)
            if end <= D:
                query[:inner, spot] = product
                query_power = query_power + folded(product)
            elif end <= 2 * D:
                key[:rows, spot] = product
                key_power = key_power + folded(product)
            else:
                value[:rows, spot] = product.astype(jnp.bfloat16)
        return norm(query_power), norm(key_power)

    def heads_of(bands, query_norm, key_norm, biases, finish):
        rows = bands * BAND
        inner = (bands - 2) * BAND

        def one_head(h, carry):
            lanes = pl.ds(pl.multiple_of(h * HEAD_DIM, HEAD_DIM), HEAD_DIM)
            head_query = (query[:inner, lanes] * query_norm * (gain_query_ref[:, lanes] * SCALE)).astype(jnp.bfloat16)
            head_key = (key[:rows, lanes] * key_norm * gain_key_ref[:, lanes]).astype(jnp.bfloat16)
            head_value = jnp.concatenate(
                [value[:rows, lanes], jnp.ones((rows, HEAD_DIM), jnp.bfloat16)], axis=1
            )
            for band in range(bands - 2):
                attended = attend(head_query, head_key, head_value, band * BAND, biases[band])
                finish(band, lanes, attended.astype(jnp.float32))
            return carry

        lax.fori_loop(0, HEADS, one_head, 0, unroll=HEADS)

    query_norm, key_norm = project(normed_ref, 5, True)

    biases = []
    for band in range(3):
        flags = window_ref[band * HELD + BAND : (band + 1) * HELD, : 3 * BAND].astype(jnp.float32)
        biases.append(bias_row(flags[0:1], flags[1:2]))

    for band in range(3):
        gates[band : band + 1, :] = mod_row(mod_ref, 2, level_of(levels, 0, frame - PER_SECTION + band - 1))
    gates[3:4, :] = mod_row(mod_ref, 2, level_of(levels, 1, frame))

    def finish_first(band, lanes, attended):
        gate = gates[band : band + 1, lanes]
        held = window_ref[band * HELD : band * HELD + BAND, lanes]
        moved = (held.astype(jnp.float32) + gate * attended).astype(jnp.bfloat16)
        entering = jnp.where(frame + band - 1 < PER_SECTION, held, moved)
        advanced[band * BAND : (band + 1) * BAND, lanes] = entering

    heads_of(5, query_norm, key_norm, biases, finish_first)

    for band in range(3):
        rows = slice(band * BAND, (band + 1) * BAND)
        normed[rows, :] = modulated(advanced[rows, :], mod_ref, level_of(levels, 1, frame + band - 1))

    query_norm, key_norm = project(normed, 3, False)

    bias_second = bias_row(
        jnp.where(bounds[0, 0] >= frame, 1.0, 0.0), jnp.where(bounds[0, 1] <= frame + 1, 1.0, 0.0)
    )

    def finish_second(band, lanes, attended):
        gate = gates[3:4, lanes]
        held = advanced[BAND : 2 * BAND, lanes].astype(jnp.float32)
        out_ref[:, lanes] = (held + gate * attended).astype(jnp.bfloat16)

    heads_of(3, query_norm, key_norm, [bias_second], finish_second)


def prepared(place, levels, table, around):
    smem = pl.BlockSpec(memory_space=pltpu.SMEM)
    vmem = pl.BlockSpec(memory_space=pltpu.VMEM)
    return pl.pallas_call(
        prepare,
        out_shape=[
            jax.ShapeDtypeStruct((5 * BAND, D), jnp.bfloat16),
            jax.ShapeDtypeStruct((3 * HELD, D), jnp.bfloat16),
        ],
        in_specs=[smem] * 2 + [vmem] * 2,
        out_specs=[vmem] * 2,
        compiler_params=pltpu.CompilerParams(vmem_limit_bytes=16 * 1024 * 1024),
        cost_estimate=pl.CostEstimate(flops=10_000_000, bytes_accessed=4_000_000, transcendentals=0),
        name="normed_window",
    )(place, levels, table, around)


def two_steps(place, levels, bounds, table, normed, window, gain_query, gain_key, gathered):
    smem = pl.BlockSpec(memory_space=pltpu.SMEM)
    vmem = pl.BlockSpec(memory_space=pltpu.VMEM)
    anywhere = pl.BlockSpec(memory_space=pl.ANY)
    return pl.pallas_call(
        compute,
        out_shape=jax.ShapeDtypeStruct((BAND, D), jnp.bfloat16),
        in_specs=[smem] * 3 + [vmem] * 5 + [anywhere],
        out_specs=vmem,
        scratch_shapes=[
            pltpu.VMEM((8, 2 * ROWS, 3 * D), jnp.bfloat16),
            pltpu.VMEM((3 * BAND, D), jnp.float32),
            pltpu.VMEM((5 * BAND, D), jnp.float32),
            pltpu.VMEM((5 * BAND, D), jnp.bfloat16),
            pltpu.VMEM((3 * BAND, D), jnp.bfloat16),
            pltpu.VMEM((3 * BAND, D), jnp.bfloat16),
            pltpu.VMEM((8, D), jnp.float32),
            pltpu.SemaphoreType.DMA((6,)),
        ],
        compiler_params=pltpu.CompilerParams(vmem_limit_bytes=48 * 1024 * 1024),
        cost_estimate=pl.CostEstimate(
            flops=12_000_000_000, bytes_accessed=20_000_000, transcendentals=2_000_000
        ),
        name="two_steps",
    )(place, levels, bounds, table, normed, window, gain_query, gain_key, gathered)


def tied(value, *others):
    return lax.optimization_barrier((value, *others))[0]


def shards(
    stream, incoming, levels, bounds, mod_table, w_query, w_key, w_value, gain_query, gain_key
):
    core = lax.axis_index("core")
    frame = lax.axis_index(AXES)
    zh = lax.axis_index("zh")
    place = jnp.stack([frame, zh]).astype(jnp.int32)

    parity = lax.rem(lax.axis_index("x"), 2)
    half = jnp.where(
        core == 0,
        jnp.concatenate([w_query, w_key[:, : HALF - D]], axis=1),
        jnp.concatenate([w_key[:, HALF - D :], w_value], axis=1),
    )
    quarter = lax.dynamic_slice_in_dim(tied(half), parity * (HALF // 2), HALF // 2, axis=1)
    mirror = [(2 * zl + side, 2 * (3 - zl) + 1 - side) for zl in range(4) for side in range(2)]
    opposite = lax.ppermute(quarter, ("zl", "zh"), mirror)
    ring = [(i, (i + 1) % 4) for i in range(4)]
    beside = [(2 * i, 2 * j) for i, j in ring] + [(2 * j + 1, 2 * i + 1) for i, j in ring]
    neighbour = lax.ppermute(opposite, ("x", "core"), beside)
    stream, incoming, bounds = lax.optimization_barrier((stream, incoming, bounds, quarter))[:3]
    row = lax.broadcasted_iota(jnp.int32, (FLAGS, D), 0)
    flags = jnp.where(row == 0, bounds[0, 0] >= frame, bounds[0, 1] <= frame + 1).astype(jnp.bfloat16)
    y = lax.axis_index("y")
    last = frame >= DEVICES - PER_SECTION
    mine = jnp.where(last, incoming, stream)
    flagged = lambda block: jnp.concatenate([block, flags], axis=0)
    held = flagged(mine)

    def moved(block, distance):
        route = [(d, (d + distance) % DEVICES) for d in range(DEVICES)]
        return lax.ppermute(block, AXES, route)

    two_before = moved(held, 2)
    two_after = moved(flagged(jnp.where(last & (y > 0), incoming, stream)), -2)
    neighbour = tied(neighbour, two_before, two_after)
    other = jnp.where(
        parity == 0,
        jnp.concatenate([opposite, neighbour], axis=1),
        jnp.concatenate([neighbour, opposite], axis=1),
    )
    both = jnp.where(
        zh == 0, jnp.concatenate([half, other], axis=0), jnp.concatenate([other, half], axis=0)
    )
    gathered = lax.all_gather(both, ("y", "core"), axis=0, tiled=True)

    given = jnp.concatenate([held, jnp.where(zh == 1, two_before, two_after)], axis=0)
    taken = lax.ppermute(tied(given, opposite), "zh", [(0, 1), (1, 0)])
    around = moved(jnp.concatenate([two_before, two_after, held, taken], axis=0), PER_SECTION)

    table = mod_table.transpose(1, 0, 2).reshape(3 * LEVELS, D)
    normed, window = prepared(place, levels, table, around)
    return two_steps(
        place,
        levels,
        bounds,
        table,
        normed,
        window,
        gain_query[None, :],
        gain_key[None, :],
        gathered.reshape(8, 2, 2 * ROWS, HALF),
    )


def solution(mesh):
    inner = Mesh(mesh.devices.reshape(SHAPE), AXES)
    queue_dp = P(AXES, None)
    dp = P(("y", "zh"), None)
    in_specs = (queue_dp, dp, P(), queue_dp, P(), dp, dp, dp, P(), P())
    return jax.shard_map(shards, mesh=inner, in_specs=in_specs, out_specs=queue_dp, check_vma=False)
```
